256 devices in a mesh: row: 32 (over z, x), col: 4 (over y), rhs: 2 (over core).
Axes of the slice: x: 4, y: 4, z: 8, core: 2. Of those that a mesh axis runs over, the one named last changes fastest.
Arguments:
- vector: bfloat16 [64, 262144], P('rhs', ('row', 'col')), may hold values from -6 to 6
- near_blocks: bfloat16 [1024, 8, 256, 256], P(('row', 'col'), 'rhs'), may hold values from -0.125 to 0.125
- near_cols: int32 [1024, 8], P(('row', 'col'), 'rhs'), may hold values from 0 to 1023, as said below
- coupling: bfloat16 [32, 4, 32, 2, 128, 128], P('row', 'col'), may hold values from -0.1875 to 0.1875
- far_dst: int32 [32, 4, 32, 2], P('row', 'col'), may hold values from 0 to 31
- far_src: int32 [32, 4, 32, 2], P('row', 'col'), may hold values from 0 to 7
- row_cluster_basis: bfloat16 [1024, 256, 128], P(('row', 'col')), may hold values from -0.5 to 0.5
- column_cluster_basis: bfloat16 [1024, 256, 128], P(('row', 'col')), may hold values from -0.375 to 0.375
Outputs:
- first_image: bfloat16 [64, 262144], P('rhs', ('row', 'col'))
- second_image: bfloat16 [64, 262144], P('rhs', ('row', 'col'))
The draws below stay inside these ranges and needn't reach their ends.
Inputs may be any that keep to these rules, and one draw needn't show every extreme that they name: near_cols[c, 0] = c, and every entry lies within 8 of its row's cluster c.
All inputs are finite; a program needn't handle non-finite values.
Results may differ from the reference program's by a relative error of at most 0.02.
Values may be sent and summed in bfloat16 or wider, within the bound.
No kernel may reach another device: no remote copies, remote signals or barrier semaphores. Data moves between devices by JAX's collectives and lax.ppermute only.
A program may use at most 64 MiB of HBM per device.

```python
import jax
import jax.numpy as jnp
from jax import lax

LEAF = 256
K = 128
R = 64
CPD = 8
NEAR = 8
FPP = 2
NC = 1024
N = 262144
N_ROW = 32
N_COL = 4


def draw_near_cols(key, part):
    offsets = jax.random.randint(key, (NC, NEAR), -CPD, CPD + 1)
    offsets = offsets.at[:, 0].set(0)
    anchor = jnp.arange(NC, dtype=jnp.int32)[:, None]
    return jnp.clip(anchor + offsets, 0, NC - 1).astype(jnp.int32)


def draw_far_dst(key, part):
    values = jax.random.randint(key, (N_ROW, N_COL, N_ROW, FPP), 0, CPD * N_COL)
    values = values.at[:, :, 0, 0].set(CPD * N_COL - 1)
    values = values.at[:, :, N_ROW - 1, FPP - 1].set(0)
    return values.astype(jnp.int32)


def draw_far_src(key, part):
    values = jax.random.randint(key, (N_ROW, N_COL, N_ROW, FPP), 0, CPD)
    values = values.at[:, :, 0, 0].set(CPD - 1)
    values = values.at[:, :, N_ROW - 1, FPP - 1].set(0)
    return values.astype(jnp.int32)


def levels(rng, extent, split, least, top_value):
    factor_of, own = 1.0, jax.random.fold_in(rng, 6)
    for dim, parts in split:
        steps = jnp.exp(jax.random.uniform(jax.random.fold_in(own, dim), (parts,), jnp.float32, least / len(split), top_value / len(split)))
        factor_of = factor_of * jnp.repeat(steps, extent[dim] // parts).reshape([-1 if axis == dim else 1 for axis in range(len(extent))])
    return factor_of


def noise(stream_key, extent, width, reach, cuts=(), kind=jnp.bfloat16):
    gain = levels(stream_key, extent, cuts, -0.22, 0.18) if cuts else 1.0
    result = jax.random.normal(stream_key, extent, jnp.float32) * width * gain
    return jnp.minimum(jnp.maximum(result, -reach), reach).astype(kind)


def setup_inputs(seed: int = 0) -> dict:
    splits = jax.random.split(jax.random.key(seed), 9)
    vector = noise(splits[0], (R, N), 1.0, 6.0, ((0, 2), (1, 128)))
    near_blocks = noise(splits[1], (NC, NEAR, LEAF, LEAF), (LEAF * NEAR) ** -0.5, 0.125, ((0, 128), (1, 2)))
    near_cols = draw_near_cols(jax.random.fold_in(splits[8], 71), 0)
    coupling = noise(splits[3], (N_ROW, N_COL, N_ROW, FPP, K, K), (K * max(N_ROW * FPP // CPD, 1)) ** -0.5, 0.1875, ((0, 32), (1, 4)))
    far_dst = draw_far_dst(jax.random.fold_in(splits[8], 71), 0)
    far_src = draw_far_src(jax.random.fold_in(splits[8], 71), 0)
    row_cluster_basis = noise(splits[6], (NC, LEAF, K), K ** -0.5, 0.5, ((0, 128),))
    column_cluster_basis = noise(splits[7], (NC, LEAF, K), LEAF ** -0.5, 0.375, ((0, 128),))
    return {"vector": vector, "near_blocks": near_blocks, "near_cols": near_cols, "coupling": coupling, "far_dst": far_dst, "far_src": far_src, "row_cluster_basis": row_cluster_basis, "column_cluster_basis": column_cluster_basis}


def apply_operator(vector, near_blocks, near_cols, coupling, far_dst, far_src, row_cluster_basis, column_cluster_basis):
    columns = vector.reshape(R, NC, LEAF).astype(jnp.float32)
    cluster_leading_order = jnp.transpose(columns, (1, 0, 2))
    coefficient_array = jnp.einsum('baj,bjt->bat', cluster_leading_order, column_cluster_basis.astype(jnp.float32), precision=lax.Precision.HIGHEST).astype(jnp.bfloat16)
    coeff_wide = coefficient_array.astype(jnp.float32)
    owned_rows = CPD * N_COL
    col_ids = jnp.arange(N_COL, dtype=jnp.int32)[:, None, None]
    peer_ids = jnp.arange(N_ROW, dtype=jnp.int32)[None, :, None]

    def far_row(item):
        block_list, targets, sources = item
        global_src = ((peer_ids * N_COL + col_ids) * CPD + sources).reshape(-1).astype(jnp.int32)
        picked = coeff_wide[global_src]
        contrib = jnp.einsum('bhm,bkm->bhk', picked, block_list.reshape(-1, K, K).astype(jnp.float32), precision=lax.Precision.HIGHEST)
        return jax.ops.segment_sum(contrib, targets.reshape(-1).astype(jnp.int32), num_segments=owned_rows)

    coupled_terms = lax.map(far_row, (coupling, far_dst, far_src)).reshape(NC, R, K).astype(jnp.bfloat16)
    group_blocks = near_blocks.reshape(NC // CPD, CPD, NEAR, LEAF, LEAF)
    group_cols = near_cols.reshape(NC // CPD, CPD, NEAR)

    def near_group(item):
        block_list, idents = item
        taken = cluster_leading_order[idents.astype(jnp.int32)]
        return jnp.einsum('csrm,cslm->crl', taken, block_list.astype(jnp.float32), precision=lax.Precision.HIGHEST)

    near_part = lax.map(near_group, (group_blocks, group_cols)).reshape(NC, R, LEAF)
    distant_contribution = jnp.einsum('gyu,gxu->gyx', coupled_terms.astype(jnp.float32), row_cluster_basis.astype(jnp.float32), precision=lax.Precision.HIGHEST)
    total = 0.5 * cluster_leading_order + near_part + distant_contribution
    return jnp.transpose(total, (1, 0, 2)).reshape(R, NC * LEAF).astype(jnp.bfloat16)


def reference(vector, near_blocks, near_cols, coupling, far_dst, far_src, row_cluster_basis, column_cluster_basis):
    first_image = apply_operator(vector, near_blocks, near_cols, coupling, far_dst, far_src, row_cluster_basis, column_cluster_basis)
    second_image = apply_operator(first_image, near_blocks, near_cols, coupling, far_dst, far_src, row_cluster_basis, column_cluster_basis)
    return (first_image, second_image)
```

```python
import jax
import jax.numpy as jnp
from jax import lax
from jax.sharding import PartitionSpec as P


def per_device(
    vector,
    near_blocks,
    near_cols,
    coupling,
    far_dst,
    far_src,
    row_cluster_basis,
    column_cluster_basis,
):
    clusters, leaf_size, basis_rank = row_cluster_basis.shape
    row_peers = lax.axis_size("row")
    col_peers = lax.axis_size("col")
    slot_count = far_src.shape[3]
    pairs = row_peers * slot_count
    own_cols = vector.shape[0]
    couple = coupling.reshape(pairs, basis_rank, basis_rank)
    targets = far_dst.reshape(pairs)
    owned_rows = clusters * col_peers
    onehot = (targets[None, :] == jnp.arange(owned_rows, dtype=jnp.int32)[:, None]).astype(
        jnp.float32
    )
    wanted = lax.all_to_all(far_src.reshape(row_peers, slot_count), "row", 0, 0)
    wanted = wanted.reshape(pairs)

    other = [(0, 1), (1, 0)]
    first_cluster = (lax.axis_index(("row", "col")) - 1) * clusters
    local_cols = near_cols - first_cluster
    far_cols = lax.ppermute(local_cols, "rhs", other)
    far_blocks = lax.ppermute(near_blocks, "rhs", other)
    col = lax.axis_index("col")
    line = row_peers * col_peers
    up = [(i, i + 1) for i in range(line - 1)]
    down = [(j, i) for i, j in up]

    def apply_once(current):
        before = lax.ppermute(current[:, -clusters * leaf_size :], ("row", "col"), up)
        after = lax.ppermute(current[:, : clusters * leaf_size], ("row", "col"), down)
        window = jnp.concatenate([before, current, after], axis=1)
        window = window.reshape(own_cols, 3 * clusters, leaf_size)

        def near_of(cols, blocks):
            taken = jnp.take(window, cols, axis=1, mode="clip")
            return jnp.einsum("hcsm,cslm->hcl", taken, blocks, preferred_element_type=jnp.float32)

        near = near_of(local_cols, near_blocks) + near_of(far_cols, far_blocks)

        leaves = current.reshape(own_cols, clusters, leaf_size)
        coeffs = jnp.einsum(
            "sao,aon->asn", leaves, column_cluster_basis, preferred_element_type=jnp.float32
        ).astype(jnp.bfloat16)
        packed = jnp.take(coeffs, wanted, axis=0, mode="clip")
        packed = packed.reshape(row_peers, slot_count * own_cols, basis_rank)
        picked = lax.all_to_all(packed, "row", 0, 0).reshape(pairs, own_cols, basis_rank)
        contrib = jnp.einsum("bhm,bkm->bhk", picked, couple, preferred_element_type=jnp.float32)
        sums = jnp.einsum("ib,bhk->ihk", onehot, contrib, precision=lax.Precision.HIGHEST)
        sums = sums.astype(jnp.bfloat16).reshape(
            col_peers, clusters * own_cols, basis_rank
        )
        total = lax.dynamic_index_in_dim(sums, col, 0, keepdims=False).astype(jnp.float32)
        for step in range(1, col_peers):
            part = lax.dynamic_index_in_dim(
                sums, lax.rem(col + step, col_peers), 0, keepdims=False
            )
            ring = [(i, (i + step) % col_peers) for i in range(col_peers)]
            total = total + lax.ppermute(part, "col", ring).astype(jnp.float32)
        coupled = total.astype(jnp.bfloat16).reshape(clusters, own_cols, basis_rank)
        distant = jnp.einsum(
            "oba,oya->boy", coupled, row_cluster_basis, preferred_element_type=jnp.float32
        )
        image = 0.5 * leaves.astype(jnp.float32) + near + distant
        return image.astype(jnp.bfloat16).reshape(own_cols, clusters * leaf_size)

    first_image = apply_once(vector)
    second_image = apply_once(first_image)
    return (first_image, second_image)


def solution(mesh):
    return jax.shard_map(
        per_device,
        mesh=mesh,
        in_specs=(
            P("rhs", ("row", "col")),
            P(("row", "col"), "rhs", None, None),
            P(("row", "col"), "rhs"),
            P("row", "col", None, None, None, None),
            P("row", "col", None, None),
            P("row", "col", None, None),
            P(("row", "col"), None, None),
            P(("row", "col"), None, None),
        ),
        out_specs=(P("rhs", ("row", "col")), P("rhs", ("row", "col"))),
        check_vma=False,
    )
```

```python
import functools

import jax
import jax.numpy as jnp
from jax import lax
from jax.experimental import pallas as pl
from jax.experimental.pallas import tpu as pltpu
from jax.sharding import PartitionSpec as P

SMEM = pl.BlockSpec(memory_space=pltpu.SMEM)
VMEM = pl.BlockSpec(memory_space=pltpu.VMEM)
HBM = pl.BlockSpec(memory_space=pltpu.HBM)
NN = (((1,), (0,)), ((), ()))
NT = (((1,), (1,)), ((), ()))


def in_hbm(x):
    return pltpu.with_memory_space_constraint(x, pltpu.HBM)


def pinned(x):
    return pltpu.with_memory_space_constraint(x, pltpu.VMEM)


def product(a, b, dims=NT):
    return lax.dot_general(a, b, dims, preferred_element_type=jnp.float32)


def params(mib):
    return pltpu.CompilerParams(vmem_limit_bytes=mib * 2**20)


def cost(flops, moved):
    return pl.CostEstimate(flops=flops, bytes_accessed=moved, transcendentals=0)


def stage_kernel(*refs):
    count = (len(refs) - 1) // 3
    sources, turned, held = (refs[k * count : (k + 1) * count] for k in range(3))
    sems = refs[-1]
    copies = []
    for source, hold in zip(sources, held):
        for k in range(source.shape[0]):
            sem = sems.at[len(copies)]
            copies.append(pltpu.make_async_copy(source.at[k], hold.at[k], sem))
    for copy in copies:
        copy.start()
    at = 0
    for source, out, hold in zip(sources, turned, held):
        for k in range(source.shape[0]):
            copies[at].wait()
            at += 1
            for n in range(source.shape[1]):
                out[k, n] = hold[k, n].T


def stage(*arrays):
    size = sum(x.size * x.dtype.itemsize for x in arrays)
    return pl.pallas_call(
        stage_kernel,
        out_shape=[pltpu.VMEM(x.shape, x.dtype) for x in arrays],
        in_specs=[HBM] * len(arrays),
        out_specs=[VMEM] * len(arrays),
        scratch_shapes=[pltpu.VMEM(x.shape, x.dtype) for x in arrays]
        + [pltpu.SemaphoreType.DMA((sum(x.shape[0] for x in arrays),))],
        compiler_params=params(20),
        cost_estimate=cost(0, 2 * size),
        name="stage",
    )(*[pltpu.with_memory_space_constraint(x, pltpu.HBM) for x in arrays])


def pick_into(wanted_ref, coeffs_ref, packed_ref):
    peers, slots = wanted_ref.shape[0], wanted_ref.shape[2]
    batch = 8
    for at in range(0, peers * slots, batch):
        taken = [
            coeffs_ref[wanted_ref[b // slots, 0, b % slots]] for b in range(at, at + batch)
        ]
        for k, block in enumerate(taken):
            packed_ref[at + k] = block


def pick(wanted, coeffs):
    pairs = wanted.shape[0] * wanted.shape[2]
    return pl.pallas_call(
        pick_into,
        out_shape=pltpu.VMEM((pairs, *coeffs.shape[1:]), coeffs.dtype),
        in_specs=[SMEM, VMEM],
        out_specs=VMEM,
        compiler_params=params(4),
        cost_estimate=cost(0, 600_000),
        name="pick",
    )(wanted, coeffs)


def couple_kernel(place_ref, target_ref, picked_ref, couple_ref, own_ref, *rest):
    parts, total = rest[:-1], rest[-1]
    clusters = own_ref.shape[0]
    peers = len(parts) + 1
    total[...] = jnp.zeros_like(total)
    slots = target_ref.shape[0]
    for b in range(picked_ref.shape[0]):
        row = target_ref[b % slots, b // slots]
        block = couple_ref[b // slots, b % slots]
        total[row] = total[row] + product(picked_ref[b], block, NN)
    place = place_ref[0]
    own_ref[...] = total[pl.ds(place * clusters, clusters)]
    for step, part in enumerate(parts, 1):
        at = lax.rem(place + step, peers) * clusters
        part[...] = total[pl.ds(at, clusters)].astype(part.dtype)


def couple_and_add(place, targets, picked, couple, clusters, peers):
    pairs, cols, rank = picked.shape
    part = jax.ShapeDtypeStruct((clusters, cols, rank), picked.dtype)
    return pl.pallas_call(
        couple_kernel,
        out_shape=[jax.ShapeDtypeStruct(part.shape, jnp.float32)] + [part] * (peers - 1),
        in_specs=[SMEM, SMEM, VMEM, VMEM],
        out_specs=[VMEM] * peers,
        scratch_shapes=[pltpu.VMEM((clusters * peers, cols, rank), jnp.float32)],
        compiler_params=params(8),
        cost_estimate=cost(2 * pairs * cols * rank * rank, 4_000_000),
        name="couple",
    )(place, targets, picked, pinned(couple))


def near_kernel(
    first_ref, here, there, before, current, after, a_ref, b_ref, out_ref,
    window, a_held, b_held, turned, sems,
):
    clusters, slots, leaf = a_ref.shape[0], a_ref.shape[1], a_ref.shape[2]
    width = current.shape[1]
    copies = []
    for c in range(clusters):
        for source, held in ((a_ref, a_held), (b_ref, b_held)):
            copies.append(
                pltpu.make_async_copy(source.at[c], held.at[c], sems.at[len(copies)])
            )
    for copy in copies:
        copy.start()
    for k, piece in enumerate((before, current, after)):
        window[:, k * width : (k + 1) * width] = piece[...]
    first = first_ref[0]
    for c in range(clusters):
        total = 0.5 * current[:, c * leaf : (c + 1) * leaf].astype(jnp.float32)
        for k, (cols, held) in enumerate(((here, a_held), (there, b_held))):
            copies[2 * c + k].wait()
            for s in range(slots):
                block = turned.at[c % 2, k * slots + s]
                block[...] = held[c, s].T
                start = pl.multiple_of((cols[s, c] - first) * leaf, leaf)
                total = total + product(window[:, pl.ds(start, leaf)], block[...], NN)
        out_ref[c] = total


def near_terms(first, here, there, before, current, after, a, b):
    clusters, slots, leaf, _ = a.shape
    cols, width = current.shape
    return pl.pallas_call(
        near_kernel,
        out_shape=jax.ShapeDtypeStruct((clusters, cols, leaf), jnp.float32),
        in_specs=[SMEM] * 3 + [VMEM] * 3 + [HBM] * 2,
        out_specs=VMEM,
        scratch_shapes=[
            pltpu.VMEM((cols, 3 * width), current.dtype),
            pltpu.VMEM(a.shape, a.dtype),
            pltpu.VMEM(b.shape, b.dtype),
            pltpu.VMEM((2, 2 * slots, leaf, leaf), a.dtype),
            pltpu.SemaphoreType.DMA((2 * clusters,)),
        ],
        compiler_params=params(16),
        cost_estimate=cost(4 * clusters * slots * cols * leaf * leaf, 9_000_000),
        name="near",
    )(first, here, there, before, current, after, in_hbm(a), in_hbm(b))


def image_into(c, own, parts, row_basis, near, image):
    leaf = row_basis.shape[1]
    total = own[c]
    for part in parts:
        total = total + part[c].astype(jnp.float32)
    coupled = total.astype(image.dtype)
    at = slice(c * leaf, (c + 1) * leaf)
    value = near[c] + product(coupled, row_basis[c])
    value = value.astype(image.dtype)
    image[:, at] = value
    return value


def last_kernel(own, *refs):
    *parts, row_basis, near, image = refs
    for c in range(own.shape[0]):
        image_into(c, own, parts, row_basis, near, image)


def middle_kernel(wanted_ref, own, *refs):
    *parts, row_basis, near, column_basis, image, packed, coeffs = refs
    for c in range(own.shape[0]):
        value = image_into(c, own, parts, row_basis, near, image)
        coeffs[c] = product(value, column_basis[c], NN).astype(coeffs.dtype)
    pick_into(wanted_ref, coeffs, packed)


def finish(own, parts, row_basis, near):
    clusters, cols, _ = own.shape
    dtype = row_basis.dtype
    return pl.pallas_call(
        last_kernel,
        out_shape=jax.ShapeDtypeStruct((cols, clusters * row_basis.shape[1]), dtype),
        in_specs=[VMEM] * (len(parts) + 3),
        out_specs=VMEM,
        compiler_params=params(8),
        cost_estimate=cost(20_000_000, 1_500_000),
        name="finish",
    )(own, *parts, row_basis, near)


def finish_and_pick(wanted, own, parts, row_basis, near, column_basis):
    clusters, cols, rank = own.shape
    pairs = wanted.shape[0] * wanted.shape[2]
    dtype = row_basis.dtype
    return pl.pallas_call(
        middle_kernel,
        out_shape=[
            jax.ShapeDtypeStruct((cols, clusters * row_basis.shape[1]), dtype),
            jax.ShapeDtypeStruct((pairs, cols, rank), dtype),
        ],
        in_specs=[SMEM] + [VMEM] * (len(parts) + 4),
        out_specs=[VMEM, VMEM],
        scratch_shapes=[pltpu.VMEM((clusters, cols, rank), dtype)],
        compiler_params=params(8),
        cost_estimate=cost(40_000_000, 2_500_000),
        name="finish_and_pick",
    )(wanted, own, *parts, row_basis, near, column_basis)


def per_device(
    vector,
    near_blocks,
    near_cols,
    coupling,
    far_dst,
    far_src,
    row_cluster_basis,
    column_cluster_basis,
):
    clusters, leaf_size, basis_rank = row_cluster_basis.shape
    row_peers = lax.axis_size("row")
    col_peers = lax.axis_size("col")
    slot_count = far_src.shape[3]
    pairs = row_peers * slot_count
    own_cols = vector.shape[0]
    wanted = lax.all_to_all(far_src.reshape(row_peers, 1, slot_count), "row", 0, 0, tiled=True)

    other = [(0, 1), (1, 0)]
    first = ((lax.axis_index(("row", "col")) - 1) * clusters).astype(jnp.int32).reshape(1)
    our_cols = near_cols.T
    their_cols = lax.ppermute(our_cols, "rhs", other)
    targets = far_dst.reshape(row_peers, slot_count).T
    place = lax.axis_index("col").astype(jnp.int32).reshape(1)
    line = row_peers * col_peers
    up = [(i, i + 1) for i in range(line - 1)]
    down = [(j, i) for i, j in up]

    leaves = vector.reshape(own_cols, clusters, leaf_size)
    coeffs = jnp.einsum(
        "sao,aon->asn", leaves, column_cluster_basis, preferred_element_type=jnp.float32
    ).astype(jnp.bfloat16)
    couple = stage(coupling.reshape(row_peers, slot_count, basis_rank, basis_rank))[0]
    theirs = lax.ppermute(near_blocks, "rhs", other)
    wanted, their_cols = lax.optimization_barrier((wanted, their_cols))
    packed = pick(wanted, coeffs)

    def exchanges(current, packed):
        packed, current = lax.optimization_barrier((packed, current))
        before = lax.ppermute(current, ("row", "col"), up)
        after = lax.ppermute(current, ("row", "col"), down)
        blocks = packed.reshape(row_peers, slot_count * own_cols, basis_rank)
        picked = lax.all_to_all(blocks, "row", 0, 0, tiled=True)
        picked = picked.reshape(pairs, own_cols, basis_rank)
        own, *parts = couple_and_add(place, targets, picked, couple, clusters, col_peers)
        near = near_terms(
            first, our_cols, their_cols, before, current, after, near_blocks, theirs
        )
        moved = []
        for step, part in enumerate(parts, 1):
            ring = [(i, (i + step) % col_peers) for i in range(col_peers)]
            moved.append(lax.ppermute(part, "col", ring))
        return own, moved, near

    own, parts, near = exchanges(vector, packed)
    first_image, packed = finish_and_pick(
        wanted, own, parts, row_cluster_basis, near, column_cluster_basis
    )
    own, parts, near = exchanges(first_image, packed)
    second_image = finish(own, parts, row_cluster_basis, near)
    return (first_image, second_image)


def solution(mesh):
    return jax.shard_map(
        per_device,
        mesh=mesh,
        in_specs=(
            P("rhs", ("row", "col")),
            P(("row", "col"), "rhs", None, None),
            P(("row", "col"), "rhs"),
            P("row", "col", None, None, None, None),
            P("row", "col", None, None),
            P("row", "col", None, None),
            P(("row", "col"), None, None),
            P(("row", "col"), None, None),
        ),
        out_specs=(P("rhs", ("row", "col")), P("rhs", ("row", "col"))),
        check_vma=False,
    )
```

```python
import jax
import jax.numpy as jnp
from jax import lax
from jax.experimental import pallas as pl
from jax.experimental.pallas import tpu as pltpu
from jax.sharding import PartitionSpec as P

SMEM = pl.BlockSpec(memory_space=pltpu.SMEM)
VMEM = pl.BlockSpec(memory_space=pltpu.VMEM)
HBM = pl.BlockSpec(memory_space=pltpu.HBM)
NN = (((1,), (0,)), ((), ()))
NT = (((1,), (1,)), ((), ()))


def in_hbm(x):
    return pltpu.with_memory_space_constraint(x, pltpu.HBM)


def pinned(x):
    return pltpu.with_memory_space_constraint(x, pltpu.VMEM)


def product(a, b, dims=NT):
    return lax.dot_general(a, b, dims, preferred_element_type=jnp.float32)


def params(mib):
    return pltpu.CompilerParams(vmem_limit_bytes=mib * 2**20)


def cost(flops, moved):
    return pl.CostEstimate(flops=flops, bytes_accessed=moved, transcendentals=0)


def stage_kernel(*refs):
    count = (len(refs) - 1) // 3
    sources, turned, held = (refs[k * count : (k + 1) * count] for k in range(3))
    sems = refs[-1]
    copies = []
    for source, hold in zip(sources, held):
        for k in range(source.shape[0]):
            sem = sems.at[len(copies)]
            copies.append(pltpu.make_async_copy(source.at[k], hold.at[k], sem))
    for copy in copies:
        copy.start()
    at = 0
    for source, out, hold in zip(sources, turned, held):
        for k in range(source.shape[0]):
            copies[at].wait()
            at += 1
            for n in range(source.shape[1]):
                out[k, n] = hold[k, n].T


def stage(*arrays):
    size = sum(x.size * x.dtype.itemsize for x in arrays)
    return pl.pallas_call(
        stage_kernel,
        out_shape=[pltpu.VMEM(x.shape, x.dtype) for x in arrays],
        in_specs=[HBM] * len(arrays),
        out_specs=[VMEM] * len(arrays),
        scratch_shapes=[pltpu.VMEM(x.shape, x.dtype) for x in arrays]
        + [pltpu.SemaphoreType.DMA((sum(x.shape[0] for x in arrays),))],
        compiler_params=params(20),
        cost_estimate=cost(0, 2 * size),
        name="stage",
    )(*[pltpu.with_memory_space_constraint(x, pltpu.HBM) for x in arrays])


def pick_into(wanted_ref, coeffs_ref, packed_ref):
    peers, slots = wanted_ref.shape[0], wanted_ref.shape[2]
    batch = 8
    for at in range(0, peers * slots, batch):
        taken = [
            coeffs_ref[wanted_ref[b // slots, 0, b % slots]] for b in range(at, at + batch)
        ]
        for k, block in enumerate(taken):
            packed_ref[at + k] = block


def pick(wanted, coeffs):
    pairs = wanted.shape[0] * wanted.shape[2]
    return pl.pallas_call(
        pick_into,
        out_shape=pltpu.VMEM((pairs, *coeffs.shape[1:]), coeffs.dtype),
        in_specs=[SMEM, VMEM],
        out_specs=VMEM,
        compiler_params=params(4),
        cost_estimate=cost(0, 600_000),
        name="pick",
    )(wanted, coeffs)


def couple_kernel(place_ref, target_ref, picked_ref, couple_ref, own_ref, *rest):
    parts, total = rest[:-1], rest[-1]
    clusters = own_ref.shape[0]
    peers = len(parts) + 1
    total[...] = jnp.zeros_like(total)
    slots = target_ref.shape[0]
    for b in range(picked_ref.shape[0]):
        row = target_ref[b % slots, b // slots]
        block = couple_ref[b // slots, b % slots]
        total[row] = total[row] + product(picked_ref[b], block, NN)
    place = place_ref[0]
    own_ref[...] = total[pl.ds(place * clusters, clusters)]
    for step, part in enumerate(parts, 1):
        at = lax.rem(place + step, peers) * clusters
        part[...] = total[pl.ds(at, clusters)].astype(part.dtype)


def couple_and_add(place, targets, picked, couple, clusters, peers):
    pairs, cols, rank = picked.shape
    part = jax.ShapeDtypeStruct((clusters, cols, rank), picked.dtype)
    return pl.pallas_call(
        couple_kernel,
        out_shape=[jax.ShapeDtypeStruct(part.shape, jnp.float32)] + [part] * (peers - 1),
        in_specs=[SMEM, SMEM, VMEM, VMEM],
        out_specs=[VMEM] * peers,
        scratch_shapes=[pltpu.VMEM((clusters * peers, cols, rank), jnp.float32)],
        compiler_params=params(8),
        cost_estimate=cost(2 * pairs * cols * rank * rank, 4_000_000),
        name="couple",
    )(place, targets, picked, pinned(couple))


def near_kernel(
    first_ref, here, there, before, after, current_ref, a_ref, b_ref, out_ref,
    window, a_held, b_held, turned, sems,
):
    clusters, slots, leaf = a_ref.shape[0], a_ref.shape[1], a_ref.shape[2]
    width = before.shape[1]
    middle = pltpu.make_async_copy(
        current_ref, window.at[:, pl.ds(width, width)], sems.at[2 * clusters]
    )
    middle.start()
    copies = []
    for c in range(clusters):
        for source, held in ((a_ref, a_held), (b_ref, b_held)):
            copies.append(
                pltpu.make_async_copy(source.at[c], held.at[c], sems.at[len(copies)])
            )
    for copy in copies:
        copy.start()
    window[:, :width] = before[...]
    window[:, 2 * width :] = after[...]
    first = first_ref[0]
    middle.wait()
    for c in range(clusters):
        at = width + c * leaf
        total = 0.5 * window[:, at : at + leaf].astype(jnp.float32)
        for k, (cols, held) in enumerate(((here, a_held), (there, b_held))):
            copies[2 * c + k].wait()
            for s in range(slots):
                block = turned.at[c % 2, k * slots + s]
                block[...] = held[c, s].T
                start = pl.multiple_of((cols[s, c] - first) * leaf, leaf)
                total = total + product(window[:, pl.ds(start, leaf)], block[...], NN)
        out_ref[c] = total


def near_terms(first, here, there, before, current, after, a, b):
    clusters, slots, leaf, _ = a.shape
    cols, width = current.shape
    return pl.pallas_call(
        near_kernel,
        out_shape=jax.ShapeDtypeStruct((clusters, cols, leaf), jnp.float32),
        in_specs=[SMEM] * 3 + [VMEM] * 2 + [HBM] * 3,
        out_specs=VMEM,
        scratch_shapes=[
            pltpu.VMEM((cols, 3 * width), current.dtype),
            pltpu.VMEM(a.shape, a.dtype),
            pltpu.VMEM(b.shape, b.dtype),
            pltpu.VMEM((2, 2 * slots, leaf, leaf), a.dtype),
            pltpu.SemaphoreType.DMA((2 * clusters + 1,)),
        ],
        compiler_params=params(16),
        cost_estimate=cost(4 * clusters * slots * cols * leaf * leaf, 9_000_000),
        name="near",
    )(first, here, there, before, after, in_hbm(current), in_hbm(a), in_hbm(b))


def image_into(c, own, parts, row_basis, near, image):
    leaf = row_basis.shape[1]
    total = own[c]
    for part in parts:
        total = total + part[c].astype(jnp.float32)
    coupled = total.astype(image.dtype)
    at = slice(c * leaf, (c + 1) * leaf)
    value = near[c] + product(coupled, row_basis[c])
    value = value.astype(image.dtype)
    image[:, at] = value
    return value


def last_kernel(own, *refs):
    *parts, row_basis, near, image = refs
    for c in range(own.shape[0]):
        image_into(c, own, parts, row_basis, near, image)


def middle_kernel(wanted_ref, own, *refs):
    *parts, row_basis, near, column_basis, image, packed, coeffs = refs
    for c in range(own.shape[0]):
        value = image_into(c, own, parts, row_basis, near, image)
        coeffs[c] = product(value, column_basis[c], NN).astype(coeffs.dtype)
    pick_into(wanted_ref, coeffs, packed)


def finish(own, parts, row_basis, near):
    clusters, cols, _ = own.shape
    dtype = row_basis.dtype
    return pl.pallas_call(
        last_kernel,
        out_shape=jax.ShapeDtypeStruct((cols, clusters * row_basis.shape[1]), dtype),
        in_specs=[VMEM] * (len(parts) + 3),
        out_specs=VMEM,
        compiler_params=params(8),
        cost_estimate=cost(20_000_000, 1_500_000),
        name="finish",
    )(own, *parts, row_basis, near)


def finish_and_pick(wanted, own, parts, row_basis, near, column_basis):
    clusters, cols, rank = own.shape
    pairs = wanted.shape[0] * wanted.shape[2]
    dtype = row_basis.dtype
    return pl.pallas_call(
        middle_kernel,
        out_shape=[
            jax.ShapeDtypeStruct((cols, clusters * row_basis.shape[1]), dtype),
            pltpu.HBM((pairs, cols, rank), dtype),
        ],
        in_specs=[SMEM] + [VMEM] * (len(parts) + 4),
        out_specs=[VMEM, VMEM],
        scratch_shapes=[pltpu.VMEM((clusters, cols, rank), dtype)],
        compiler_params=params(8),
        cost_estimate=cost(40_000_000, 2_500_000),
        name="finish_and_pick",
    )(wanted, own, *parts, row_basis, near, column_basis)


def per_device(
    vector,
    near_blocks,
    near_cols,
    coupling,
    far_dst,
    far_src,
    row_cluster_basis,
    column_cluster_basis,
):
    clusters, leaf_size, basis_rank = row_cluster_basis.shape
    row_peers = lax.axis_size("row")
    col_peers = lax.axis_size("col")
    slot_count = far_src.shape[3]
    pairs = row_peers * slot_count
    own_cols = vector.shape[0]
    wanted = lax.all_to_all(far_src.reshape(row_peers, 1, slot_count), "row", 0, 0, tiled=True)

    other = [(0, 1), (1, 0)]
    first = ((lax.axis_index(("row", "col")) - 1) * clusters).astype(jnp.int32).reshape(1)
    our_cols = near_cols.T
    their_cols = lax.ppermute(our_cols, "rhs", other)
    targets = far_dst.reshape(row_peers, slot_count).T
    place = lax.axis_index("col").astype(jnp.int32).reshape(1)
    line = row_peers * col_peers
    up = [(i, i + 1) for i in range(line - 1)]
    down = [(j, i) for i, j in up]

    leaves = vector.reshape(own_cols, clusters, leaf_size)
    coeffs = jnp.einsum(
        "sao,aon->asn", leaves, column_cluster_basis, preferred_element_type=jnp.float32
    ).astype(jnp.bfloat16)
    couple = stage(coupling.reshape(row_peers, slot_count, basis_rank, basis_rank))[0]
    theirs = lax.ppermute(near_blocks, "rhs", other)
    wanted, their_cols = lax.optimization_barrier((wanted, their_cols))
    packed = pick(wanted, coeffs)

    def exchanges(current, packed):
        packed, current = lax.optimization_barrier((packed, current))
        before = lax.ppermute(current, ("row", "col"), up)
        after = lax.ppermute(current, ("row", "col"), down)
        blocks = packed.reshape(row_peers, slot_count * own_cols, basis_rank)
        picked = lax.all_to_all(blocks, "row", 0, 0, tiled=True)
        picked = picked.reshape(pairs, own_cols, basis_rank)
        own, *parts = couple_and_add(place, targets, picked, couple, clusters, col_peers)
        near = near_terms(
            first, our_cols, their_cols, before, current, after, near_blocks, theirs
        )
        moved = []
        for step in (1, 3, 2):
            part = parts[step - 1]
            ring = [(i, (i + step) % col_peers) for i in range(col_peers)]
            moved.append(lax.ppermute(part, "col", ring))
        return own, moved, near

    own, parts, near = exchanges(vector, packed)
    first_image, packed = finish_and_pick(
        wanted, own, parts, row_cluster_basis, near, column_cluster_basis
    )
    own, parts, near = exchanges(first_image, packed)
    second_image = finish(own, parts, row_cluster_basis, near)
    return (first_image, second_image)


def solution(mesh):
    return jax.shard_map(
        per_device,
        mesh=mesh,
        in_specs=(
            P("rhs", ("row", "col")),
            P(("row", "col"), "rhs", None, None),
            P(("row", "col"), "rhs"),
            P("row", "col", None, None, None, None),
            P("row", "col", None, None),
            P("row", "col", None, None),
            P(("row", "col"), None, None),
            P(("row", "col"), None, None),
        ),
        out_specs=(P("rhs", ("row", "col")), P("rhs", ("row", "col"))),
        check_vma=False,
    )
```

```python
import jax
import jax.numpy as jnp
from jax import lax
from jax.experimental import pallas as pl
from jax.experimental.pallas import tpu as pltpu
from jax.sharding import PartitionSpec as P

SMEM = pl.BlockSpec(memory_space=pltpu.SMEM)
VMEM = pl.BlockSpec(memory_space=pltpu.VMEM)
HBM = pl.BlockSpec(memory_space=pltpu.HBM)
NN = (((1,), (0,)), ((), ()))
NT = (((1,), (1,)), ((), ()))


def in_hbm(x):
    return pltpu.with_memory_space_constraint(x, pltpu.HBM)


def pinned(x):
    return pltpu.with_memory_space_constraint(x, pltpu.VMEM)


def product(a, b, dims=NT):
    return lax.dot_general(a, b, dims, preferred_element_type=jnp.float32)


def params(mib):
    return pltpu.CompilerParams(vmem_limit_bytes=mib * 2**20)


def cost(flops, moved):
    return pl.CostEstimate(flops=flops, bytes_accessed=moved, transcendentals=0)


def stage_kernel(*refs):
    count = (len(refs) - 1) // 3
    sources, turned, held = (refs[k * count : (k + 1) * count] for k in range(3))
    sems = refs[-1]
    copies = []
    for source, hold in zip(sources, held):
        for k in range(source.shape[0]):
            sem = sems.at[len(copies)]
            copies.append(pltpu.make_async_copy(source.at[k], hold.at[k], sem))
    for copy in copies:
        copy.start()
    at = 0
    for source, out, hold in zip(sources, turned, held):
        for k in range(source.shape[0]):
            copies[at].wait()
            at += 1
            for n in range(source.shape[1]):
                out[k, n] = hold[k, n].T


def stage(*arrays):
    size = sum(x.size * x.dtype.itemsize for x in arrays)
    return pl.pallas_call(
        stage_kernel,
        out_shape=[pltpu.VMEM(x.shape, x.dtype) for x in arrays],
        in_specs=[HBM] * len(arrays),
        out_specs=[VMEM] * len(arrays),
        scratch_shapes=[pltpu.VMEM(x.shape, x.dtype) for x in arrays]
        + [pltpu.SemaphoreType.DMA((sum(x.shape[0] for x in arrays),))],
        compiler_params=params(20),
        cost_estimate=cost(0, 2 * size),
        name="stage",
    )(*[pltpu.with_memory_space_constraint(x, pltpu.HBM) for x in arrays])


def pick_into(wanted_ref, coeffs_ref, packed_ref):
    peers, slots = wanted_ref.shape[0], wanted_ref.shape[2]
    batch = 8
    for at in range(0, peers * slots, batch):
        taken = [
            coeffs_ref[wanted_ref[b // slots, 0, b % slots]] for b in range(at, at + batch)
        ]
        for k, block in enumerate(taken):
            packed_ref[at + k] = block


def pick(wanted, coeffs):
    pairs = wanted.shape[0] * wanted.shape[2]
    return pl.pallas_call(
        pick_into,
        out_shape=pltpu.VMEM((pairs, *coeffs.shape[1:]), coeffs.dtype),
        in_specs=[SMEM, VMEM],
        out_specs=VMEM,
        compiler_params=params(4),
        cost_estimate=cost(0, 600_000),
        name="pick",
    )(wanted, coeffs)


def couple_kernel(place_ref, target_ref, picked_ref, couple_ref, own_ref, *rest):
    parts, total = rest[:-1], rest[-1]
    clusters = own_ref.shape[0]
    peers = len(parts) + 1
    total[...] = jnp.zeros_like(total)
    slots = target_ref.shape[0]
    for b in range(picked_ref.shape[0]):
        row = target_ref[b % slots, b // slots]
        block = couple_ref[b // slots, b % slots]
        total[row] = total[row] + product(picked_ref[b], block, NN)
    place = place_ref[0]
    own_ref[...] = total[pl.ds(place * clusters, clusters)]
    for step, part in enumerate(parts, 1):
        at = lax.rem(place + step, peers) * clusters
        part[...] = total[pl.ds(at, clusters)].astype(part.dtype)


def couple_and_add(place, targets, picked, couple, clusters, peers):
    pairs, cols, rank = picked.shape
    part = jax.ShapeDtypeStruct((clusters, cols, rank), picked.dtype)
    return pl.pallas_call(
        couple_kernel,
        out_shape=[jax.ShapeDtypeStruct(part.shape, jnp.float32)] + [part] * (peers - 1),
        in_specs=[SMEM, SMEM, VMEM, VMEM],
        out_specs=[VMEM] * peers,
        scratch_shapes=[pltpu.VMEM((clusters * peers, cols, rank), jnp.float32)],
        compiler_params=params(8),
        cost_estimate=cost(2 * pairs * cols * rank * rank, 4_000_000),
        name="couple",
    )(place, targets, picked, pinned(couple))


def near_kernel(
    first_ref, here, there, before, after, current_ref, a_ref, b_ref, out_ref,
    window, a_held, b_held, turned, sems,
):
    clusters, slots, leaf = a_ref.shape[0], a_ref.shape[1], a_ref.shape[2]
    width = before.shape[1]
    middle = pltpu.make_async_copy(
        current_ref, window.at[:, pl.ds(width, width)], sems.at[2 * clusters]
    )
    middle.start()
    copies = []
    for c in range(clusters):
        for source, held in ((a_ref, a_held), (b_ref, b_held)):
            copies.append(
                pltpu.make_async_copy(source.at[c], held.at[c], sems.at[len(copies)])
            )
    for copy in copies:
        copy.start()
    window[:, :width] = before[...]
    window[:, 2 * width :] = after[...]
    first = first_ref[0]
    middle.wait()
    for c in range(clusters):
        at = width + c * leaf
        total = 0.5 * window[:, at : at + leaf].astype(jnp.float32)
        copies[2 * c].wait()
        copies[2 * c + 1].wait()
        for k, (cols, held) in enumerate(((here, a_held), (there, b_held))):
            for s in range(slots):
                block = turned.at[c % 4, k * slots + s]
                block[...] = held[c, s].T
                start = pl.multiple_of((cols[s, c] - first) * leaf, leaf)
                total = total + product(window[:, pl.ds(start, leaf)], block[...], NN)
        out_ref[c] = total


def near_terms(first, here, there, before, current, after, a, b):
    clusters, slots, leaf, _ = a.shape
    cols, width = current.shape
    return pl.pallas_call(
        near_kernel,
        out_shape=jax.ShapeDtypeStruct((clusters, cols, leaf), jnp.float32),
        in_specs=[SMEM] * 3 + [VMEM] * 2 + [HBM] * 3,
        out_specs=VMEM,
        scratch_shapes=[
            pltpu.VMEM((cols, 3 * width), current.dtype),
            pltpu.VMEM(a.shape, a.dtype),
            pltpu.VMEM(b.shape, b.dtype),
            pltpu.VMEM((4, 2 * slots, leaf, leaf), a.dtype),
            pltpu.SemaphoreType.DMA((2 * clusters + 1,)),
        ],
        compiler_params=params(20),
        cost_estimate=cost(4 * clusters * slots * cols * leaf * leaf, 9_000_000),
        name="near",
    )(first, here, there, before, after, in_hbm(current), in_hbm(a), in_hbm(b))


def image_into(c, own, parts, row_basis, near, image):
    leaf = row_basis.shape[1]
    total = own[c]
    for part in parts:
        total = total + part[c].astype(jnp.float32)
    coupled = total.astype(image.dtype)
    at = slice(c * leaf, (c + 1) * leaf)
    value = near[c] + product(coupled, row_basis[c])
    value = value.astype(image.dtype)
    image[:, at] = value
    return value


def last_kernel(own, *refs):
    *parts, row_basis, near, image = refs
    for c in range(own.shape[0]):
        image_into(c, own, parts, row_basis, near, image)


def middle_kernel(wanted_ref, own, *refs):
    *parts, row_basis, near, column_basis, image, packed, coeffs = refs
    for c in range(own.shape[0]):
        value = image_into(c, own, parts, row_basis, near, image)
        coeffs[c] = product(value, column_basis[c], NN).astype(coeffs.dtype)
    pick_into(wanted_ref, coeffs, packed)


def finish(own, parts, row_basis, near):
    clusters, cols, _ = own.shape
    dtype = row_basis.dtype
    return pl.pallas_call(
        last_kernel,
        out_shape=jax.ShapeDtypeStruct((cols, clusters * row_basis.shape[1]), dtype),
        in_specs=[VMEM] * (len(parts) + 3),
        out_specs=VMEM,
        compiler_params=params(8),
        cost_estimate=cost(20_000_000, 1_500_000),
        name="finish",
    )(own, *parts, row_basis, near)


def finish_and_pick(wanted, own, parts, row_basis, near, column_basis):
    clusters, cols, rank = own.shape
    pairs = wanted.shape[0] * wanted.shape[2]
    dtype = row_basis.dtype
    return pl.pallas_call(
        middle_kernel,
        out_shape=[
            jax.ShapeDtypeStruct((cols, clusters * row_basis.shape[1]), dtype),
            pltpu.HBM((pairs, cols, rank), dtype),
        ],
        in_specs=[SMEM] + [VMEM] * (len(parts) + 4),
        out_specs=[VMEM, VMEM],
        scratch_shapes=[pltpu.VMEM((clusters, cols, rank), dtype)],
        compiler_params=params(8),
        cost_estimate=cost(40_000_000, 2_500_000),
        name="finish_and_pick",
    )(wanted, own, *parts, row_basis, near, column_basis)


def per_device(
    vector,
    near_blocks,
    near_cols,
    coupling,
    far_dst,
    far_src,
    row_cluster_basis,
    column_cluster_basis,
):
    clusters, leaf_size, basis_rank = row_cluster_basis.shape
    row_peers = lax.axis_size("row")
    col_peers = lax.axis_size("col")
    slot_count = far_src.shape[3]
    pairs = row_peers * slot_count
    own_cols = vector.shape[0]
    wanted = lax.all_to_all(far_src.reshape(row_peers, 1, slot_count), "row", 0, 0, tiled=True)

    other = [(0, 1), (1, 0)]
    first = ((lax.axis_index(("row", "col")) - 1) * clusters).astype(jnp.int32).reshape(1)
    our_cols = near_cols.T
    their_cols = lax.ppermute(our_cols, "rhs", other)
    targets = far_dst.reshape(row_peers, slot_count).T
    place = lax.axis_index("col").astype(jnp.int32).reshape(1)
    line = row_peers * col_peers
    up = [(i, i + 1) for i in range(line - 1)]
    down = [(j, i) for i, j in up]

    leaves = vector.reshape(own_cols, clusters, leaf_size)
    coeffs = jnp.einsum(
        "sao,aon->asn", leaves, column_cluster_basis, preferred_element_type=jnp.float32
    ).astype(jnp.bfloat16)
    couple = stage(coupling.reshape(row_peers, slot_count, basis_rank, basis_rank))[0]
    theirs = lax.ppermute(near_blocks, "rhs", other)
    wanted, their_cols = lax.optimization_barrier((wanted, their_cols))
    packed = pick(wanted, coeffs)

    def exchanges(current, packed):
        packed, current = lax.optimization_barrier((packed, current))
        before = lax.ppermute(current, ("row", "col"), up)
        after = lax.ppermute(current, ("row", "col"), down)
        blocks = packed.reshape(row_peers, slot_count * own_cols, basis_rank)
        picked = lax.all_to_all(blocks, "row", 0, 0, tiled=True)
        picked = picked.reshape(pairs, own_cols, basis_rank)
        own, *parts = couple_and_add(place, targets, picked, couple, clusters, col_peers)
        near = near_terms(
            first, our_cols, their_cols, before, current, after, near_blocks, theirs
        )
        moved = []
        for step in (1, 3, 2):
            part = parts[step - 1]
            ring = [(i, (i + step) % col_peers) for i in range(col_peers)]
            moved.append(lax.ppermute(part, "col", ring))
        return own, moved, near

    own, parts, near = exchanges(vector, packed)
    first_image, packed = finish_and_pick(
        wanted, own, parts, row_cluster_basis, near, column_cluster_basis
    )
    own, parts, near = exchanges(first_image, packed)
    second_image = finish(own, parts, row_cluster_basis, near)
    return (first_image, second_image)


def solution(mesh):
    return jax.shard_map(
        per_device,
        mesh=mesh,
        in_specs=(
            P("rhs", ("row", "col")),
            P(("row", "col"), "rhs", None, None),
            P(("row", "col"), "rhs"),
            P("row", "col", None, None, None, None),
            P("row", "col", None, None),
            P("row", "col", None, None),
            P(("row", "col"), None, None),
            P(("row", "col"), None, None),
        ),
        out_specs=(P("rhs", ("row", "col")), P("rhs", ("row", "col"))),
        check_vma=False,
    )
```
